32 devices in a mesh: dp: 8 (over y, x, core), heads: 4 (over z).
Axes of the slice: x: 2, y: 2, z: 4, core: 2. Of those that a mesh axis runs over, the one named last changes fastest.
Arguments:
- latents_in: bfloat16 [32, 64, 1024], P('dp'), may hold values from -6 to 6
- media_tokens: bfloat16 [32, 8, 256, 1024], P('dp'), may hold values from -6 to 6
- frame_counts: int32 [32], P('dp'), may hold values from 1 to 8, as said below
- time_embed: bfloat16 [8, 1024], replicated, may hold values from -3 to 3
- media_gain: bfloat16 [1024], replicated, may hold values from 0.5 to 1.5
- media_bias: bfloat16 [1024], replicated, may hold values from -1.75 to 1.75
- latent_gain: bfloat16 [1024], replicated, may hold values from 0.5 to 1.5
- latent_bias: bfloat16 [1024], replicated, may hold values from -1.75 to 1.75
- ff_gain: bfloat16 [1024], replicated, may hold values from 0.5 to 1.5
- ff_bias: bfloat16 [1024], replicated, may hold values from -1.75 to 1.75
- w_query: bfloat16 [1024, 512], P(None, 'heads'), may hold values from -0.1875 to 0.1875
- w_key: bfloat16 [1024, 512], P(None, 'heads'), may hold values from -0.1875 to 0.1875
- w_value: bfloat16 [1024, 512], P(None, 'heads'), may hold values from -0.1875 to 0.1875
- w_out: bfloat16 [512, 1024], P('heads'), may hold values from -3 to 3
- w_up: bfloat16 [1024, 4096], replicated, may hold values from -0.1875 to 0.1875
- w_down: bfloat16 [4096, 1024], replicated, may hold values from -0.09375 to 0.09375
- cotangent: bfloat16 [32, 64, 1024], P('dp'), may hold values from -6 to 6
Outputs:
- latents_out: bfloat16 [32, 64, 1024], P('dp')
- grad_latents: bfloat16 [32, 64, 1024], P('dp')
- grad_media: bfloat16 [32, 8, 256, 1024], P('dp', None, 'heads')
- grad_time: float32 [8, 1024], replicated
- grad_media_gain: float32 [1024], replicated
- grad_media_bias: float32 [1024], replicated
- grad_latent_gain: float32 [1024], replicated
- grad_latent_bias: float32 [1024], replicated
- grad_ff_gain: float32 [1024], replicated
- grad_ff_bias: float32 [1024], replicated
- grad_query: float32 [1024, 512], P(None, 'heads')
- grad_key: float32 [1024, 512], P(None, 'heads')
- grad_value: float32 [1024, 512], P(None, 'heads')
- grad_out: float32 [512, 1024], P('heads')
- grad_up: float32 [1024, 4096], P('dp')
- grad_down: float32 [4096, 1024], P('dp')
The draws below stay inside these ranges and needn't reach their ends.
Inputs may be any that keep to these rules, and one draw needn't show every extreme that they name: `frame_counts`: some clip has 8 frames and some clip has 1.
All inputs are finite; a program needn't handle non-finite values.
Results may differ from the reference program's by a relative error of at most 0.012.
The reference program's roundings to bfloat16 on the way count: a program that leaves them out, or rounds other values in their place, can miss the bound.
Values may be sent and summed in bfloat16 or wider, within the bound.
No kernel may reach another device: no remote copies, remote signals or barrier semaphores. Data moves between devices by JAX's collectives and lax.ppermute only.
A program may use at most 256 MiB of HBM per device.

```python
import jax
import jax.numpy as jnp
from jax import lax

D = 1024
HEADS = 8
HEAD_DIM = 64
FF = 4096
LATENTS = 64
FRAMES = 8
PATCHES = 256
INNER = 512
CLIPS = 32


def draw_frame_counts(key, part):
    key = jax.random.fold_in(key, 7)
    first_key, second_key = jax.random.split(key)
    counted = jax.random.randint(first_key, (CLIPS,), 1, FRAMES + 1)
    order = jax.random.permutation(second_key, CLIPS)
    counted = counted.at[order[0]].set(FRAMES)
    counted = counted.at[order[1]].set(1)
    return counted.astype(jnp.int32)


def block_scale(key, dims, cuts, smallest, top_value):
    loudness, own = 1.0, jax.random.fold_in(key, 6)
    for position, blocks in cuts:
        heights = jnp.exp(jax.random.uniform(jax.random.fold_in(own, position), (blocks,), jnp.float32, smallest / len(cuts), top_value / len(cuts)))
        loudness = loudness * jnp.repeat(heights, dims[position] // blocks).reshape([-1 if axis == position else 1 for axis in range(len(dims))])
    return loudness


def normal_values(key, extent, deviation, reach, cuts=(), held_as=jnp.bfloat16):
    values = deviation * jax.random.normal(key, extent, jnp.float32)
    if cuts:
        values = values * block_scale(key, extent, cuts, -0.22, 0.18)
    return jnp.clip(values, -reach, reach).astype(held_as)


def setup_inputs(seed: int = 0) -> dict:
    streams_of = jax.random.split(jax.random.key(seed), 18)
    return {
        "latents_in": normal_values(streams_of[0], (CLIPS, LATENTS, D), 1.0, 6.0, ((0, 8),)),
        "media_tokens": normal_values(streams_of[1], (CLIPS, FRAMES, PATCHES, D), 1.0, 6.0, ((0, 8),)),
        "frame_counts": draw_frame_counts(jax.random.fold_in(streams_of[17], 71), 0),
        "time_embed": normal_values(streams_of[3], (FRAMES, D), 0.5, 3.0),
        "media_gain": jnp.clip(1.0 + 0.1 * jax.random.normal(streams_of[4], (D,), jnp.float32), 0.5, 1.5).astype(jnp.bfloat16),
        "media_bias": normal_values(streams_of[5], (D,), 0.3, 1.75),
        "latent_gain": jnp.clip(1.0 + 0.1 * jax.random.normal(streams_of[6], (D,), jnp.float32), 0.5, 1.5).astype(jnp.bfloat16),
        "latent_bias": normal_values(streams_of[7], (D,), 0.3, 1.75),
        "ff_gain": jnp.clip(1.0 + 0.1 * jax.random.normal(streams_of[8], (D,), jnp.float32), 0.5, 1.5).astype(jnp.bfloat16),
        "ff_bias": normal_values(streams_of[9], (D,), 0.3, 1.75),
        "w_query": normal_values(streams_of[10], (D, INNER), D ** -0.5, 0.1875, ((1, 4),)),
        "w_key": normal_values(streams_of[11], (D, INNER), D ** -0.5, 0.1875, ((1, 4),)),
        "w_value": normal_values(streams_of[12], (D, INNER), D ** -0.5, 0.1875, ((1, 4),)),
        "w_out": normal_values(streams_of[13], (INNER, D), 0.5, 3.0, ((0, 4),)),
        "w_up": normal_values(streams_of[14], (D, FF), D ** -0.5, 0.1875),
        "w_down": normal_values(streams_of[15], (FF, D), FF ** -0.5, 0.09375),
        "cotangent": normal_values(streams_of[16], (CLIPS, LATENTS, D), 1.0, 6.0, ((0, 8),)),
    }


@jax.custom_vjp
def low(v):
    return lax.optimization_barrier(v.astype(jnp.bfloat16)).astype(jnp.float32)

@jax.custom_vjp
def low_back(v):
    return v

def low_keep(v):
    return (low(v), None)

def low_pass(kept, grad):
    return (grad,)

def back_keep(v):
    return (v, None)

def back_low(kept, grad):
    return (low(grad),)
low.defvjp(low_keep, low_pass)
low_back.defvjp(back_keep, back_low)

def layer_norm(values, gain_values, bias_values):
    row_mean = lax.optimization_barrier(jnp.mean(values, axis=-1, keepdims=True))
    centred = values - row_mean
    inv_scale = lax.rsqrt(lax.optimization_barrier(jnp.mean(centred * centred, axis=-1, keepdims=True)) + 1e-05)
    return centred * inv_scale * gain_values + bias_values

def one_clip(params, per_clip):
    time_embed, media_gain, media_bias, latent_gain, latent_bias, ff_gain, ff_bias, w_query, w_key, w_value, w_out, w_up, w_down = params
    latents, media_clip, count = per_clip
    highest = lax.Precision.HIGHEST
    shifted = media_clip + time_embed[:, None, :]
    normed_media = low(layer_norm(shifted, media_gain, media_bias)).reshape(FRAMES * PATCHES, D)
    normed_lat = low(layer_norm(latents, latent_gain, latent_bias))
    key_rows = jnp.concatenate([normed_media, normed_lat], axis=0)
    queries = low_back(low(jnp.dot(normed_lat, w_query, precision=highest) * HEAD_DIM ** (-0.5)))
    queries = queries.reshape(LATENTS, HEADS, HEAD_DIM)
    all_keys = low_back(low(jnp.dot(key_rows, w_key, precision=highest))).reshape(-1, HEADS, HEAD_DIM)
    all_values = low_back(low(jnp.dot(key_rows, w_value, precision=highest))).reshape(-1, HEADS, HEAD_DIM)
    scores = low_back(jnp.einsum('lhe,khe->hlk', queries, all_keys, precision=highest))
    media_frame = jnp.arange(FRAMES * PATCHES, dtype=jnp.int32) // PATCHES
    key_frame = jnp.concatenate([media_frame, jnp.zeros((LATENTS,), jnp.int32)])
    key_valid = key_frame < count
    scores = jnp.where(key_valid[None, None, :], scores, -1e+30)
    row_max = lax.optimization_barrier(jnp.max(scores, axis=-1, keepdims=True))
    expd = jnp.exp(scores - row_max)
    probs = low(expd / lax.optimization_barrier(jnp.sum(expd, axis=-1, keepdims=True)))
    attended = jnp.einsum('hlk,khe->lhe', probs, all_values, precision=highest)
    attended = low_back(low(attended)).reshape(LATENTS, INNER)
    mixed_lat = latents + low_back(jnp.dot(attended, w_out, precision=highest))
    normed_ff = low(layer_norm(mixed_lat, ff_gain, ff_bias))
    hidden = low_back(jnp.dot(normed_ff, w_up, precision=highest))
    active = low(jax.nn.gelu(hidden, approximate=False))
    return mixed_lat + jnp.dot(active, w_down, precision=highest)

def reference(latents_in, media_tokens, frame_counts, time_embed, media_gain, media_bias, latent_gain, latent_bias, ff_gain, ff_bias, w_query, w_key, w_value, w_out, w_up, w_down, cotangent):
    params = tuple((item.astype(jnp.float32) for item in (time_embed, media_gain, media_bias, latent_gain, latent_bias, ff_gain, ff_bias, w_query, w_key, w_value, w_out, w_up, w_down)))
    clip_step = jax.checkpoint(one_clip)

    def forward(latents, media_all, weights):
        return lax.map(lambda per_clip: clip_step(weights, per_clip), (latents, media_all, frame_counts))
    result, pullback = jax.vjp(forward, latents_in.astype(jnp.float32), media_tokens.astype(jnp.float32), params)
    grad_lat, grad_med, gradients = pullback(cotangent.astype(jnp.float32))
    return (result.astype(jnp.bfloat16), grad_lat.astype(jnp.bfloat16), grad_med.astype(jnp.bfloat16), gradients[0], gradients[1], gradients[2], gradients[3], gradients[4], gradients[5], gradients[6], gradients[7], gradients[8], gradients[9], gradients[10], gradients[11], gradients[12])
```

```python
import functools

import jax
import jax.numpy as jnp
from jax import lax
from jax.sharding import PartitionSpec as P

HEAD_DIM = 64
EPSILON = 1e-05
NEG_FILL = -1e30
F32 = jnp.float32
BF16 = jnp.bfloat16


def norm_parts(values):
    row_mean = jnp.mean(values, axis=-1, keepdims=True)
    centred = values - row_mean
    inv_scale = lax.rsqrt(jnp.mean(centred * centred, axis=-1, keepdims=True) + EPSILON)
    return (centred * inv_scale, inv_scale)


def norm_back(grad_normed, unit_values, inv_scale, gain_values):
    scaled = grad_normed * gain_values
    return inv_scale * (
        scaled
        - jnp.mean(scaled, axis=-1, keepdims=True)
        - unit_values * jnp.mean(scaled * unit_values, axis=-1, keepdims=True)
    )


def gelu_exact(hidden_in):
    return jax.nn.gelu(hidden_in, approximate=False)


def mm(form, a, b):
    return jnp.einsum(form, a, b, preferred_element_type=F32)


def swap(values, axis, distance):
    size = lax.axis_size(axis)
    return lax.ppermute(values, axis, [(i, i ^ distance) for i in range(size)])


def bit_of(axis, bit):
    return (lax.axis_index(axis) >> bit) & 1


def from_all(values, axis):
    return [values] + [swap(values, axis, k) for k in range(1, lax.axis_size(axis))]


def side_by_side(mine, other, axis, bit, dim):
    high = bit_of(axis, bit) == 1
    pair = jnp.stack([jnp.where(high, other, mine), jnp.where(high, mine, other)], axis=dim)
    return pair


def dp_orders():
    bits = lax.axis_size("dp").bit_length() - 1
    return [0] + list(range(1, bits)), [0] + list(range(bits - 1, 0, -1))


def scatter_sum(blocks, order):
    bits = lax.axis_size("dp").bit_length() - 1
    held = blocks.reshape([2] * bits + list(blocks.shape[1:]))
    left = list(range(bits - 1, -1, -1))
    for bit in order:
        dim = left.index(bit)
        side = bit_of("dp", bit)
        keep = lax.dynamic_index_in_dim(held, side, dim, keepdims=False)
        send = lax.dynamic_index_in_dim(held, 1 - side, dim, keepdims=False).astype(BF16)
        got = swap(send, "dp", 1 << bit)
        held = keep.astype(F32) + got.astype(F32)
        left.remove(bit)
    return held


def gather_dp(block, order):
    bits = lax.axis_size("dp").bit_length() - 1
    rows, cols = block.shape
    held = block
    have = []
    for bit in order:
        got = swap(held, "dp", 1 << bit)
        higher = sorted([b for b in have if b > bit], reverse=True)
        dim = len(higher)
        held = side_by_side(held, got, "dp", bit, dim)
        have.append(bit)
    return held.reshape((1 << bits) * rows, cols)


def sum_all(values):
    pieces = from_all(values, "heads")
    total = functools.reduce(lambda a, b: a + b, pieces)
    for bit in dp_orders()[0]:
        total = total + swap(total, "dp", 1 << bit)
    return total


def gather_weight(shard, high_bit):
    rows, cols = shard.shape
    quarter = rows // 4
    at = (bit_of("dp", high_bit) * 2 + bit_of("dp", 0)) * quarter
    part = lax.dynamic_slice_in_dim(shard, at, quarter, 0)
    pieces = jnp.stack(from_all(part, "heads"))
    pieces = side_by_side(pieces, swap(pieces, "dp", 1 << high_bit), "dp", high_bit, 1)
    pieces = side_by_side(pieces, swap(pieces, "dp", 1), "dp", 0, 2)
    return pieces.reshape(len(pieces), rows, cols)


def forward_own(latents, media, counts, time_embed, media_gain, media_bias, normed_lat, w_query, w_kv):
    clips, frames, patches, _ = media.shape
    lat_rows = latents.shape[1]
    inner = w_query.shape[1]
    heads = inner // HEAD_DIM
    shifted = media.astype(F32) + time_embed.astype(F32)[None, :, None, :]
    unit, _ = norm_parts(shifted)
    normed = (unit * media_gain + media_bias).astype(BF16).reshape(clips, frames * patches, -1)
    rows = jnp.concatenate([normed, normed_lat], axis=1)
    queries = (mm("cld,di->cli", normed_lat, w_query) * HEAD_DIM**-0.5).astype(BF16)
    kv = mm("ckd,di->cki", rows, w_kv).astype(BF16)
    keys = kv[:, :, :inner].reshape(clips, -1, heads, HEAD_DIM)
    values = kv[:, :, inner:].reshape(clips, -1, heads, HEAD_DIM)
    scores = mm("clhe,ckhe->chlk", queries.reshape(clips, lat_rows, heads, HEAD_DIM), keys)
    at = jnp.arange(rows.shape[1])
    frame = jnp.where(at < frames * patches, at // patches, 0)
    scores = jnp.where((frame[None, :] < counts[:, None])[:, None, None, :], scores, NEG_FILL)
    top = jnp.max(scores, axis=-1, keepdims=True)
    expd = jnp.exp(scores - top)
    total = jnp.sum(expd, axis=-1, keepdims=True)
    probs = expd / total
    probs_low = probs.astype(BF16)
    rest = (probs - probs_low.astype(F32)).astype(BF16)
    attended = mm("chlk,ckhe->clhe", probs_low, values).reshape(clips, lat_rows, inner)
    more = mm("chlk,ckhe->clhe", rest, values).reshape(clips, lat_rows, inner)
    high = attended.astype(BF16)
    low = (attended - high.astype(F32) + more).astype(BF16)
    return queries, high, low, top[..., 0], 1.0 / total[..., 0]


def body(
    latents_in, media_tokens, frame_counts, time_embed, media_gain, media_bias, latent_gain, latent_bias,
    ff_gain, ff_bias, w_query, w_key, w_value, w_out, w_up, w_down, cotangent,
):
    clips, frames, patches, width = media_tokens.shape
    lat_rows = latents_in.shape[1]
    inner = w_query.shape[1]
    heads_own = inner // HEAD_DIM
    parts = lax.axis_size("heads")
    place = lax.axis_index("heads")
    dp_size = lax.axis_size("dp")
    heads = heads_own * parts
    scale = HEAD_DIM**-0.5
    media_gain32, media_bias32 = media_gain.astype(F32), media_bias.astype(F32)
    latent_gain32, latent_bias32 = latent_gain.astype(F32), latent_bias.astype(F32)
    ff_gain32, ff_bias32 = ff_gain.astype(F32), ff_bias.astype(F32)

    high_bit = dp_size.bit_length() - 2
    w_kv = jnp.concatenate([w_key, w_value], axis=1)
    out_all = gather_weight(w_out, 1).reshape(parts * inner, width)
    kv_all = gather_weight(w_kv, high_bit)
    query_all = gather_weight(w_query, 1)

    latents = latents_in.astype(F32)
    lat_unit, lat_inv = norm_parts(latents)
    normed_lat = (lat_unit * latent_gain32 + latent_bias32).astype(BF16)
    queries, att_high, att_low, top, inv_total = forward_own(
        latents, media_tokens, frame_counts, time_embed, media_gain32, media_bias32, normed_lat, w_query, w_kv
    )
    att_all = jnp.concatenate(from_all(att_high, "heads"), axis=2)
    att_low_all = jnp.concatenate(from_all(att_low, "heads"), axis=2)
    query_rows = jnp.concatenate(from_all(queries, "heads"), axis=2)
    top_all = jnp.concatenate(from_all(top, "heads"), axis=1)
    inv_total_all = jnp.concatenate(from_all(inv_total, "heads"), axis=1)

    mixed = latents + mm("cli,id->cld", att_all, out_all)
    ff_unit, ff_inv = norm_parts(mixed)
    normed_ff = (ff_unit * ff_gain32 + ff_bias32).astype(BF16)
    hidden = mm("cld,df->clf", normed_ff, w_up)
    active, pull = jax.vjp(gelu_exact, hidden)
    active = active.astype(BF16)
    latents_out = (mixed + mm("clf,fd->cld", active, w_down)).astype(BF16)
    grad_active = mm("cld,fd->clf", cotangent, w_down)
    grad_hidden = pull(grad_active)[0].astype(BF16)
    grad_normed_ff = mm("clf,df->cld", grad_hidden, w_up)
    grad_ff_gain = jnp.sum(grad_normed_ff * ff_unit, axis=(0, 1))
    grad_ff_bias = jnp.sum(grad_normed_ff, axis=(0, 1))
    grad_mixed = cotangent.astype(F32) + norm_back(grad_normed_ff, ff_unit, ff_inv, ff_gain32)
    grad_branch = grad_mixed.astype(BF16)
    grad_attended = mm("cld,id->cli", grad_branch, out_all).astype(BF16)

    side = bit_of("heads", 0)
    up_half = w_up.shape[1] // 2
    down_half = width // 2
    hidden_half = lax.dynamic_slice_in_dim(grad_hidden, side * up_half, up_half, 2)
    cot_half = lax.dynamic_slice_in_dim(cotangent, side * down_half, down_half, 2)
    grad_up = mm("cld,clf->df", normed_ff, hidden_half).astype(BF16)
    grad_down = mm("clf,cld->fd", active, cot_half).astype(BF16)
    order_a, order_b = dp_orders()
    up_sum = scatter_sum(grad_up.reshape(dp_size, -1, up_half), order_a).astype(BF16)
    down_sum = scatter_sum(grad_down.reshape(dp_size, -1, down_half), order_b).astype(BF16)
    grad_up_own = side_by_side(up_sum, swap(up_sum, "heads", 1), "heads", 0, 1).reshape(len(up_sum), -1).astype(F32)
    grad_down_own = side_by_side(down_sum, swap(down_sum, "heads", 1), "heads", 0, 1).reshape(len(down_sum), -1).astype(F32)

    own = patches // parts
    media_own = lax.dynamic_slice_in_dim(media_tokens, place * own, own, 2)
    shifted = media_own.astype(F32) + time_embed.astype(F32)[None, :, None, :]
    unit, inv = norm_parts(shifted)
    unit = unit.reshape(clips, frames * own, width)
    inv = inv.reshape(clips, frames * own, 1)
    normed_own = (unit * media_gain32 + media_bias32).astype(BF16)
    chunk = clips * lat_rows // parts
    lat_from = place * chunk
    clip_at = lat_from // lat_rows

    def rows_of(values):
        return lax.dynamic_slice_in_dim(values.reshape(clips * lat_rows, -1), lat_from, chunk, 0)

    normed_lat_own = rows_of(normed_lat)
    kv_media = mm("cpd,kdi->cpki", normed_own, kv_all).astype(BF16)
    kv_lat = mm("pd,kdi->pki", normed_lat_own, kv_all).astype(BF16)
    q_heads = query_rows.reshape(clips, lat_rows, heads, HEAD_DIM)
    g_heads = grad_attended.reshape(clips, lat_rows, heads, HEAD_DIM)
    delta = jnp.sum(
        (grad_attended.astype(F32) * (att_all.astype(F32) + att_low_all.astype(F32))).reshape(
            clips, lat_rows, heads, HEAD_DIM
        ),
        axis=-1,
    ).transpose(0, 2, 1)

    def attend_back(kv, q, g, top, inv_total, delta, valid):
        clips, rows = kv.shape[:2]
        k = kv[..., :inner].reshape(clips, rows, heads, HEAD_DIM)
        v = kv[..., inner:].reshape(clips, rows, heads, HEAD_DIM)
        scores = mm("clhe,ckhe->chlk", q, k)
        probs = jnp.exp(scores - top[..., None]) * inv_total[..., None]
        if valid is not None:
            probs = jnp.where(valid[:, None, None, :], probs, 0.0)
        grad_probs = mm("clhe,ckhe->chlk", g, v)
        grad_scores = (probs * (grad_probs - delta[..., None])).astype(BF16)
        grad_q = mm("chlk,ckhe->clhe", grad_scores, k).reshape(clips, -1, heads * HEAD_DIM)
        grad_k = mm("chlk,clhe->ckhe", grad_scores, q).astype(BF16)
        grad_v = mm("chlk,clhe->ckhe", probs.astype(BF16), g).astype(BF16)
        grad_kv = jnp.concatenate(
            [grad_k.reshape(clips, rows, parts, inner), grad_v.reshape(clips, rows, parts, inner)], axis=3
        )
        return grad_q, grad_kv

    frame = jnp.arange(frames * own) // own
    valid = frame[None, :] < frame_counts[:, None]
    grad_q, grad_kv = attend_back(kv_media, q_heads, g_heads, top_all, inv_total_all, delta, valid)

    def pick(values):
        return lax.dynamic_slice_in_dim(values, clip_at, 1, 0)

    grad_q_lat, grad_kv_lat = attend_back(
        kv_lat[None], pick(q_heads), pick(g_heads), pick(top_all), pick(inv_total_all), pick(delta), None
    )
    mine = (jnp.arange(clips) == clip_at)[:, None, None]
    grad_q = (grad_q + jnp.where(mine, grad_q_lat, 0.0)).reshape(clips * lat_rows, -1)
    q_pieces = [
        lax.dynamic_slice_in_dim(grad_q, (place ^ k) * chunk, chunk, 0) for k in range(parts)
    ]
    grad_q_own = q_pieces[0]
    for k in range(1, parts):
        turned = q_pieces[k].reshape(chunk, parts, inner)[:, [j ^ k for j in range(parts)]]
        grad_q_own = grad_q_own + swap(turned.reshape(chunk, -1).astype(BF16), "heads", k).astype(F32)
    grad_q_own = grad_q_own.astype(BF16)

    flat_kv = grad_kv.reshape(clips * frames * own, -1)
    flat_kv_lat = grad_kv_lat.reshape(chunk, -1)
    grad_w_kv = mm("rd,ri->di", normed_own.reshape(-1, width), flat_kv) + mm("rd,ri->di", normed_lat_own, flat_kv_lat)
    grad_w_q = mm("rd,ri->di", normed_lat_own, grad_q_own) * scale
    grad_w_qkv = jnp.concatenate(
        [grad_w_kv.reshape(width, parts, 2 * inner), grad_w_q.reshape(width, parts, inner)], axis=2
    ).astype(BF16)
    grad_w_out = mm("cli,cld->id", att_high, grad_branch).astype(BF16)
    qkv_rows = grad_w_qkv.reshape(dp_size, -1, parts * 3 * inner)
    qkv_sum = scatter_sum(qkv_rows, order_a).reshape(-1, parts, 3 * inner)
    qkv_own = qkv_sum[:, 0]
    for k in range(1, parts):
        qkv_own = qkv_own + swap(qkv_sum[:, k].astype(BF16), "heads", k).astype(F32)
    qkv = gather_dp(qkv_own.astype(BF16), order_a[::-1]).astype(F32)
    out_sum = scatter_sum(grad_w_out.reshape(dp_size, -1, width), order_b).astype(BF16)
    grad_out = gather_dp(out_sum, order_b[::-1]).astype(F32)

    lat_back = (
        mm("rki,kdi->rd", grad_q_own.reshape(chunk, parts, inner), query_all) * scale
        + mm("rki,kdi->rd", grad_kv_lat.reshape(chunk, parts, 2 * inner), kv_all)
    )
    lat_unit_own, lat_inv_own = rows_of(lat_unit), rows_of(lat_inv)
    grad_lat_own = (rows_of(grad_mixed) + norm_back(lat_back, lat_unit_own, lat_inv_own, latent_gain32)).astype(BF16)
    lat_pieces = jnp.stack(from_all(grad_lat_own, "heads"))
    grad_latents = jnp.concatenate(
        [lax.dynamic_index_in_dim(lat_pieces, place ^ k, 0, keepdims=False) for k in range(parts)]
    ).reshape(clips, lat_rows, width)

    media_back = mm("rki,kdi->rd", flat_kv.reshape(-1, parts, 2 * inner), kv_all).reshape(clips, frames * own, width)
    grad_shifted = norm_back(media_back, unit, inv, media_gain32)
    grad_media = grad_shifted.astype(BF16).reshape(clips, frames, own, width)
    time_part = jnp.sum(grad_shifted.reshape(clips, frames, own, width), axis=(0, 2))

    def rows_sum(values):
        return jnp.sum(values.reshape(-1, width), axis=0)[None]

    small = sum_all(
        jnp.concatenate(
            [
                time_part,
                rows_sum(media_back * unit),
                rows_sum(media_back),
                rows_sum(lat_back * lat_unit_own),
                rows_sum(lat_back),
                grad_ff_gain[None] / parts,
                grad_ff_bias[None] / parts,
            ]
        )
    )
    return (
        latents_out,
        grad_latents,
        grad_media,
        small[:frames],
        *(small[frames + i] for i in range(6)),
        qkv[:, 2 * inner :],
        qkv[:, :inner],
        qkv[:, inner : 2 * inner],
        grad_out,
        grad_up_own,
        grad_down_own,
    )


def solution(mesh):
    clip, whole, column = P("dp", None, None), P(), P(None, "heads")
    media = P("dp", None, None, None)
    placed = (clip, media, P("dp")) + (whole,) * 7 + (column,) * 3 + (P("heads", None), whole, whole, clip)
    return jax.shard_map(
        body,
        mesh=mesh,
        in_specs=placed,
        out_specs=(clip, clip, P("dp", None, "heads", None))
        + (whole,) * 7
        + (column,) * 3
        + (P("heads", None), P("dp", None), P("dp", None)),
        check_vma=False,
    )
```

```python
import functools

import jax
import jax.numpy as jnp
from jax import lax
from jax.experimental import pallas as pl
from jax.experimental.pallas import tpu as pltpu
from jax.sharding import PartitionSpec as P

HEAD_DIM = 64
EPSILON = 1e-05
NEG_FILL = -1e30
F32 = jnp.float32
BF16 = jnp.bfloat16


def norm_back(grad_normed, unit_values, inv_scale, gain_values):
    scaled = grad_normed * gain_values
    return inv_scale * (
        scaled
        - jnp.mean(scaled, axis=-1, keepdims=True)
        - unit_values * jnp.mean(scaled * unit_values, axis=-1, keepdims=True)
    )


def mm(form, a, b):
    return jnp.einsum(form, a, b, preferred_element_type=F32)


def swap(values, axis, distance):
    size = lax.axis_size(axis)
    return lax.ppermute(values, axis, [(i, i ^ distance) for i in range(size)])


def bit_of(axis, bit):
    return (lax.axis_index(axis) >> bit) & 1


def from_all(values, axis):
    return [values] + [swap(values, axis, k) for k in range(1, lax.axis_size(axis))]


def side_by_side(mine, other, axis, bit, dim):
    high = bit_of(axis, bit) == 1
    pair = jnp.stack([jnp.where(high, other, mine), jnp.where(high, mine, other)], axis=dim)
    return pair


def dp_orders():
    bits = lax.axis_size("dp").bit_length() - 1
    return [0] + list(range(1, bits)), [0] + list(range(bits - 1, 0, -1))


def scatter_sum(blocks, order):
    bits = lax.axis_size("dp").bit_length() - 1
    held = blocks.reshape([2] * bits + list(blocks.shape[1:]))
    left = list(range(bits - 1, -1, -1))
    for bit in order:
        dim = left.index(bit)
        side = bit_of("dp", bit)
        keep = lax.dynamic_index_in_dim(held, side, dim, keepdims=False)
        send = lax.dynamic_index_in_dim(held, 1 - side, dim, keepdims=False).astype(BF16)
        got = swap(send, "dp", 1 << bit)
        held = keep.astype(F32) + got.astype(F32)
        left.remove(bit)
    return held


def gather_dp_blocks(block, order):
    bits = lax.axis_size("dp").bit_length() - 1
    rows, cols = block.shape
    held = block
    have = []
    for bit in order:
        got = swap(held, "dp", 1 << bit)
        higher = sorted([b for b in have if b > bit], reverse=True)
        dim = len(higher)
        held = side_by_side(held, got, "dp", bit, dim)
        have.append(bit)
    return held.reshape(1 << bits, rows, cols)


def sum_all(values):
    pieces = from_all(values, "heads")
    total = functools.reduce(lambda a, b: a + b, pieces)
    for bit in dp_orders()[0]:
        total = total + swap(total, "dp", 1 << bit)
    return total


def gather_weight(shard, bits):
    rows, cols = shard.shape
    part = shard.reshape([2] * len(bits) + [rows >> len(bits), cols])
    for bit in bits:
        part = lax.dynamic_index_in_dim(part, bit_of("dp", bit), 0, keepdims=False)
    pieces = jnp.stack(from_all(part, "heads"))
    for bit in reversed(bits):
        pieces = side_by_side(pieces, swap(pieces, "dp", 1 << bit), "dp", bit, 1)
    return pieces.reshape(len(pieces), rows, cols)


def dot(a, b, contract):
    dims = {"nn": (1, 0), "nt": (1, 1), "tn": (0, 0)}[contract]
    return lax.dot_general(a, b, (((dims[0],), (dims[1],)), ((), ())), preferred_element_type=F32)


def head_mask(heads, rows):
    shape = (heads * rows, heads * HEAD_DIM)
    row = lax.broadcasted_iota(jnp.int32, shape, 0) // rows
    col = lax.broadcasted_iota(jnp.int32, shape, 1) // HEAD_DIM
    return row == col


def spread(values, heads):
    rows = values.shape[0]
    tiled = jnp.concatenate([values] * heads, axis=0)
    return jnp.where(head_mask(heads, rows), tiled, jnp.zeros_like(tiled))


def fold(values, heads):
    rows = values.shape[0] // heads
    kept = jnp.where(head_mask(heads, rows), values, jnp.zeros_like(values))
    total = kept[:rows]
    for h in range(1, heads):
        total = total + kept[h * rows : (h + 1) * rows]
    return total


def as_lanes(column):
    rows = column.shape[0]
    return jnp.broadcast_to(column, (rows, 128)).T[:8]


def normalised(values):
    row_mean = jnp.sum(values, axis=-1, keepdims=True) * (1.0 / values.shape[-1])
    centred = values - row_mean
    inv = lax.rsqrt(jnp.sum(centred * centred, axis=-1, keepdims=True) * (1.0 / values.shape[-1]) + EPSILON)
    return centred * inv, inv


SLOTS = 4


def valid_frames(counts, clips, streams):
    def copies(slot, clip, frame):
        return [pltpu.make_async_copy(block(clip, frame), slots.at[slot], sems.at[slot]) for block, slots, sems in streams]

    def launch(slot, clip, frame):
        @pl.when(clip < clips)
        def _():
            for copy in copies(slot, clip, frame):
                copy.start()

        last = frame + 1 >= counts[jnp.minimum(clip, clips - 1)]
        return jnp.where(last, clip + 1, clip), jnp.where(last, 0, frame + 1)

    def begin():
        clip, frame = jnp.int32(0), jnp.int32(0)
        for slot in range(SLOTS - 1):
            clip, frame = launch(slot, clip, frame)
        return jnp.int32(0), clip, frame

    def step(carry):
        at, clip, frame = carry
        slot = lax.rem(at, SLOTS)
        clip, frame = launch(lax.rem(at + SLOTS - 1, SLOTS), clip, frame)
        for copy in copies(slot, 0, 0):
            copy.wait()
        return slot, (at + 1, clip, frame)

    return begin, step


def forward_kernel(
    counts, media, time_embed, gains, latents, w_query, w_kv,
    kv_out, normed_lat_out, query_out, shared_out,
    slots, normed, kv_held, in_sems, out_sems,
):
    clips, frames, patches, width = media.shape
    inner = w_query.shape[1]
    lat_rows = latents.shape[1]
    heads = inner // HEAD_DIM
    media_rows = frames * patches
    begin, step = valid_frames(counts, clips, [(lambda c, f: media.at[c, f], slots, in_sems)])

    def kv_copy(clip):
        side = lax.rem(clip, 2)
        return pltpu.make_async_copy(kv_held.at[side], kv_out.at[clip], out_sems.at[side])

    def one_clip(clip, carry):
        @pl.when(clip >= 2)
        def _():
            kv_copy(clip - 2).wait()

        kv = kv_held.at[lax.rem(clip, 2)]
        count = counts[clip]
        unit, _ = normalised(latents[clip].astype(F32))
        normed_lat = (unit * gains[2:3, :] + gains[3:4, :]).astype(BF16)
        normed_lat_out[clip] = normed_lat
        queries = (dot(normed_lat, w_query[...], "nn") * HEAD_DIM**-0.5).astype(BF16)
        query_out[clip] = queries
        kv[media_rows:] = dot(normed_lat, w_kv[...], "nn").astype(BF16)

        def one_frame(frame, carry):
            slot, carry = step(carry)
            at = pl.multiple_of(frame * patches, patches)
            shifted = slots[slot].astype(F32) + time_embed[pl.ds(frame, 1), :]
            unit, _ = normalised(shifted)
            normed[...] = (unit * gains[0:1, :] + gains[1:2, :]).astype(BF16)
            kv[pl.ds(at, patches)] = dot(normed[...], w_kv[...], "nn").astype(BF16)
            return carry

        carry = lax.fori_loop(0, count, one_frame, carry)

        def no_frame(frame, carry):
            kv[pl.ds(pl.multiple_of(frame * patches, patches), patches)] = jnp.zeros((patches, 2 * inner), BF16)
            return carry

        lax.fori_loop(count, frames, no_frame, 0)
        spread_q = spread(queries.astype(F32), heads).astype(BF16)
        scores = dot(spread_q, kv[:, :inner], "nt")
        key = lax.broadcasted_iota(jnp.int32, scores.shape, 1)
        kept = (key < count * patches) | (key >= media_rows)
        scores = jnp.where(kept, scores, NEG_FILL)
        top = jnp.max(scores, axis=-1, keepdims=True)
        expd = jnp.exp(scores - top)
        inv_total = 1.0 / jnp.sum(expd, axis=-1, keepdims=True)
        probs = expd * inv_total
        probs_low = probs.astype(BF16)
        rest = (probs - probs_low.astype(F32)).astype(BF16)
        values = kv[:, inner:]
        attended = fold(dot(probs_low, values, "nn"), heads)
        more = fold(dot(rest, values, "nn"), heads)
        high = attended.astype(BF16)
        rows = clips * lat_rows
        shared_out[pl.ds(pl.multiple_of(clip * lat_rows, lat_rows), lat_rows)] = high
        low = (attended - high.astype(F32) + more).astype(BF16)
        shared_out[pl.ds(pl.multiple_of(rows + clip * lat_rows, lat_rows), lat_rows)] = low
        terms = []
        for stat in (as_lanes(top)[:1], as_lanes(inv_total)[:1]):
            for _ in range(3):
                terms.append(stat.astype(BF16).astype(F32))
                stat = stat - terms[-1]
        terms.append(jnp.zeros((10, terms[0].shape[1]), F32))
        shared_out[pl.ds(pl.multiple_of(2 * rows + clip * 16, 16), 16)] = jnp.concatenate(terms, axis=0).astype(BF16)
        kv_copy(clip).start()
        return carry

    lax.fori_loop(0, clips, one_clip, begin())
    for clip in range(max(clips - 2, 0), clips):
        kv_copy(clip).wait()


VMEM_SPEC = pl.BlockSpec(memory_space=pltpu.VMEM)
ANY_SPEC = pl.BlockSpec(memory_space=pl.ANY)
SMEM_SPEC = pl.BlockSpec(memory_space=pltpu.SMEM)


def forward_own(latents, media, counts, time_embed, gains, w_query, w_kv):
    clips, frames, patches, width = media.shape
    lat_rows = latents.shape[1]
    inner = w_query.shape[1]
    keys = frames * patches + lat_rows
    return pl.pallas_call(
        forward_kernel,
        in_specs=[SMEM_SPEC, ANY_SPEC] + [VMEM_SPEC] * 5,
        out_specs=[ANY_SPEC] + [VMEM_SPEC] * 3,
        out_shape=[
            jax.ShapeDtypeStruct((clips, keys, 2 * inner), BF16),
            jax.ShapeDtypeStruct((clips, lat_rows, width), BF16),
            jax.ShapeDtypeStruct((clips, lat_rows, inner), BF16),
            jax.ShapeDtypeStruct((2 * clips * lat_rows + 16 * clips, inner), BF16),
        ],
        scratch_shapes=[
            pltpu.VMEM((SLOTS, patches, width), BF16),
            pltpu.VMEM((patches, width), BF16),
            pltpu.VMEM((2, keys, 2 * inner), BF16),
            pltpu.SemaphoreType.DMA((SLOTS,)),
            pltpu.SemaphoreType.DMA((2,)),
        ],
        compiler_params=pltpu.CompilerParams(vmem_limit_bytes=56 << 20),
        cost_estimate=pl.CostEstimate(
            flops=2 * clips * frames * patches * width * 2 * inner,
            bytes_accessed=4 * clips * frames * patches * width,
            transcendentals=0,
        ),
    )(counts, media, time_embed, gains, latents, w_query, w_kv)


def feed_kernel(latents, cotangent, w_out, gains, w_up, w_down, *rest):
    attended, rest = rest[:-12], rest[-12:]
    normed_out, active_out, hidden_out, result_out, mixed_out, branch_out, grad_att_out, sums_out = rest[:8]
    unit, inv, result, back = rest[8:]
    at = pl.program_id(0)
    width = latents.shape[1]

    @pl.when(at == 0)
    def _():
        joined = jnp.concatenate([block[...] for block in attended], axis=1)
        mixed = latents[...].astype(F32) + dot(joined, w_out[...], "nn")
        unit[...], inv[...] = normalised(mixed)
        normed_out[...] = (unit[...] * gains[0:1, :] + gains[1:2, :]).astype(BF16)
        result[...] = mixed
        back[...] = jnp.zeros_like(back)

    hidden = dot(normed_out[...], w_up[...], "nn")
    grad_active = dot(cotangent[...], w_down[...], "nt")
    share = 0.5 + 0.5 * lax.erf(hidden * (0.5**0.5))
    active = (hidden * share).astype(BF16)
    slope = share + hidden * (jnp.exp(hidden * hidden * -0.5) * (1.0 / (2.0 * 3.141592653589793) ** 0.5))
    grad_hidden = (grad_active * slope).astype(BF16)
    active_out[...] = active
    hidden_out[...] = grad_hidden
    result[...] += dot(active, w_down[...], "nn")
    back[...] += dot(grad_hidden, w_up[...], "nt")

    @pl.when(at == pl.num_programs(0) - 1)
    def _():
        result_out[...] = result[...].astype(BF16)
        grad = back[...]
        sums_out[...] = jnp.concatenate(
            [
                jnp.sum(grad * unit[...], axis=0, keepdims=True),
                jnp.sum(grad, axis=0, keepdims=True),
                jnp.zeros((6, width), F32),
            ],
            axis=0,
        )
        scaled = grad * gains[0:1, :]
        mean = jnp.sum(scaled, axis=-1, keepdims=True) * (1.0 / width)
        along = jnp.sum(scaled * unit[...], axis=-1, keepdims=True) * (1.0 / width)
        mixed_grad = cotangent[...].astype(F32) + inv[...] * (scaled - mean - unit[...] * along)
        mixed_out[...] = mixed_grad
        branch = mixed_grad.astype(BF16)
        branch_out[...] = branch
        grad_att_out[...] = dot(branch, w_out[...], "nt").astype(BF16)


FEED_CHUNK = 1024


def feed(latents, attended, cotangent, w_out, gains, w_up, w_down):
    rows, width = latents.shape
    hidden = w_up.shape[1]
    inner_all = w_out.shape[0]
    chunk = min(FEED_CHUNK, hidden)
    full = lambda *shape: pl.BlockSpec(shape, lambda j: (0,) * len(shape))
    columns = lambda r: pl.BlockSpec((r, chunk), lambda j: (0, j))
    shaped = jax.ShapeDtypeStruct
    return pl.pallas_call(
        feed_kernel,
        grid=(hidden // chunk,),
        in_specs=[
            full(rows, width), full(rows, width), full(inner_all, width), full(2, width),
            columns(width), pl.BlockSpec((chunk, width), lambda j: (j, 0)),
        ]
        + [full(rows, inner_all // len(attended))] * len(attended),
        out_specs=[
            full(rows, width), columns(rows), columns(rows), full(rows, width), full(rows, width),
            full(rows, width), full(rows, inner_all), full(8, width),
        ],
        out_shape=[
            shaped((rows, width), BF16), shaped((rows, hidden), BF16), shaped((rows, hidden), BF16),
            shaped((rows, width), BF16), shaped((rows, width), F32), shaped((rows, width), BF16),
            shaped((rows, inner_all), BF16), shaped((8, width), F32),
        ],
        scratch_shapes=[
            pltpu.VMEM((rows, width), F32), pltpu.VMEM((rows, 1), F32),
            pltpu.VMEM((rows, width), F32), pltpu.VMEM((rows, width), F32),
        ],
        compiler_params=pltpu.CompilerParams(vmem_limit_bytes=56 << 20),
        cost_estimate=pl.CostEstimate(
            flops=8 * rows * width * hidden, bytes_accessed=4 * width * hidden, transcendentals=2 * rows * hidden
        ),
    )(latents, cotangent, w_out, gains, w_up, w_down, *attended)


def back_block(keys, values, normed, wide_q, wide_g, top, inv_total, delta):
    scores = dot(keys, wide_q, "nt")
    probs = jnp.exp(scores - top) * inv_total
    if normed is not None:
        probs = jnp.where(normed, probs, 0.0)
    grad_probs = dot(values, wide_g, "nt")
    grad_scores = (probs * (grad_probs - delta)).astype(BF16)
    grad_keys = dot(grad_scores, wide_q, "nn").astype(BF16)
    grad_values = dot(probs.astype(BF16), wide_g, "nn").astype(BF16)
    return grad_scores, grad_keys, grad_values


def delta_lanes(grad_att, high, low, heads):
    product = grad_att.astype(F32) * (high.astype(F32) + low.astype(F32))
    return as_lanes(jnp.sum(spread(product, heads), axis=1, keepdims=True))[:1]


def stat_lanes(block):
    terms = block.astype(F32)
    return terms[0:1] + terms[1:2] + terms[2:3], terms[3:4] + terms[4:5] + terms[5:6]


def own_heads_kernel(
    counts, media, kv_all, time_embed, gains, normed_lat, queries, shared, grad_att, branch,
    lat_out, weights_out,
    slots, kv_slots, normed, lat_kv, total, grad_q, in_sems, kv_sems, lat_sem,
):
    clips, frames, patches, width = media.shape
    lat_rows, inner = queries.shape[1:]
    heads = inner // HEAD_DIM
    media_rows = frames * patches
    dp_size, _, piece = weights_out.shape
    begin, step = valid_frames(
        counts,
        clips,
        [
            (lambda c, f: media.at[c, f], slots, in_sems),
            (lambda c, f: kv_all.at[c, pl.ds(pl.multiple_of(f * patches, patches), patches)], kv_slots, kv_sems),
        ],
    )
    lat_copy = pltpu.make_async_copy(kv_all.at[:, pl.ds(media_rows, lat_rows)], lat_kv, lat_sem)
    lat_copy.start()
    carry = begin()
    total[...] = jnp.zeros_like(total)
    lat_copy.wait()

    def one_clip(clip, carry):
        rows = pl.ds(pl.multiple_of(clip * lat_rows, lat_rows), lat_rows)
        stat_rows = pl.ds(pl.multiple_of(2 * clips * lat_rows + clip * 16, 16), 16)
        high = shared[rows]
        low = shared[pl.ds(pl.multiple_of((clips + clip) * lat_rows, lat_rows), lat_rows)]
        top, inv_total = stat_lanes(shared[stat_rows])
        grad_att_rows = grad_att[rows, :inner]
        delta = delta_lanes(grad_att_rows, high, low, heads)
        wide_q = spread(queries[clip].astype(F32), heads).astype(BF16)
        wide_g = spread(grad_att_rows.astype(F32), heads).astype(BF16)
        grad_q[...] = jnp.zeros_like(grad_q)

        def one_frame(frame, carry):
            slot, carry = step(carry)
            shifted = slots[slot].astype(F32) + time_embed[pl.ds(frame, 1), :]
            unit, _ = normalised(shifted)
            normed[...] = (unit * gains[0:1, :] + gains[1:2, :]).astype(BF16)
            keys, values = kv_slots[slot, :, :inner], kv_slots[slot, :, inner:]
            grad_scores, grad_k, grad_v = back_block(keys, values, None, wide_q, wide_g, top, inv_total, delta)
            grad_q[...] += dot(grad_scores, keys, "tn")
            total[inner : 3 * inner] += dot(jnp.concatenate([grad_k, grad_v], axis=1), normed[...], "tn")
            return carry

        carry = lax.fori_loop(0, counts[clip], one_frame, carry)
        keys, values = lat_kv[clip, :, :inner], lat_kv[clip, :, inner:]
        grad_scores, grad_k, grad_v = back_block(keys, values, None, wide_q, wide_g, top, inv_total, delta)
        grad_query = fold(grad_q[...] + dot(grad_scores, keys, "tn"), heads).astype(BF16) * HEAD_DIM**-0.5
        joined = jnp.concatenate([grad_query.astype(BF16), grad_k, grad_v], axis=1)
        lat_out[rows] = joined
        total[: 3 * inner] += dot(joined, normed_lat[clip], "tn")
        total[3 * inner :] += dot(high, branch[rows], "tn")
        return carry

    lax.fori_loop(0, clips, one_clip, carry)
    for d in range(dp_size):
        for part in range(4):
            tile = total[part * inner : (part + 1) * inner, d * piece : (d + 1) * piece]
            if piece == inner and part < 3:
                tile = tile.T
            weights_out[d, part * inner : (part + 1) * inner] = tile.astype(BF16)


def own_heads_back(counts, media, kv, time_embed, gains, normed_lat, queries, shared, grad_att, branch, dp_size):
    clips, frames, patches, width = media.shape
    lat_rows, inner = queries.shape[1:]
    return pl.pallas_call(
        own_heads_kernel,
        in_specs=[SMEM_SPEC, ANY_SPEC, ANY_SPEC] + [VMEM_SPEC] * 7,
        out_specs=[VMEM_SPEC] * 2,
        out_shape=[
            jax.ShapeDtypeStruct((clips * lat_rows, 3 * inner), BF16),
            jax.ShapeDtypeStruct((dp_size, 4 * inner, width // dp_size), BF16),
        ],
        scratch_shapes=[
            pltpu.VMEM((SLOTS, patches, width), BF16),
            pltpu.VMEM((SLOTS, patches, 2 * inner), BF16),
            pltpu.VMEM((patches, width), BF16),
            pltpu.VMEM((clips, lat_rows, 2 * inner), BF16),
            pltpu.VMEM((4 * inner, width), F32),
            pltpu.VMEM((inner // HEAD_DIM * lat_rows, inner), F32),
            pltpu.SemaphoreType.DMA((SLOTS,)),
            pltpu.SemaphoreType.DMA((SLOTS,)),
            pltpu.SemaphoreType.DMA,
        ],
        compiler_params=pltpu.CompilerParams(vmem_limit_bytes=56 << 20),
        cost_estimate=pl.CostEstimate(
            flops=4 * clips * frames * patches * width * 2 * inner,
            bytes_accessed=2 * clips * frames * patches * width,
            transcendentals=0,
        ),
    )(counts, media, kv, time_embed, gains, normed_lat, queries, shared, grad_att, branch)


FRAME_GROUP = 4


def own_patches_kernel(scalars, media, time_embed, gains, weights, queries, grad_att, *rest):
    shared, (grad_out, sums_out, unit, inv, normed, back) = rest[:-6], rest[-6:]
    clip, group = pl.program_id(0), pl.program_id(1)
    parts = len(shared)
    width = media.shape[3]
    frames, own = media.shape[1:3]
    inner = weights.shape[2] // 3
    lat_rows = queries.shape[2]
    clips = pl.num_programs(0)
    joined = max(1, min(parts, 256 // inner))
    count = scalars[clip]
    first = group * frames

    @pl.when((clip == 0) & (group == 0))
    def _():
        sums_out[...] = jnp.zeros_like(sums_out)

    @pl.when(first >= count)
    def _():
        grad_out[...] = jnp.zeros_like(grad_out)

    @pl.when(first < count)
    def _():
        for f in range(frames):
            at = slice(f * own, (f + 1) * own)
            unit[at], inv[at] = normalised(media[0, f].astype(F32) + time_embed[pl.ds(first + f, 1), :])
            normed[at] = (unit[at] * gains[0:1, :] + gains[1:2, :]).astype(BF16)
        lanes = joined * inner // HEAD_DIM * lat_rows
        frame = lax.broadcasted_iota(jnp.int32, (frames * own, lanes), 0) // own + first
        kept = frame < count
        rows = pl.ds(pl.multiple_of(clip * lat_rows, lat_rows), lat_rows)
        low_rows = pl.ds(pl.multiple_of((clips + clip) * lat_rows, lat_rows), lat_rows)
        stat_rows = pl.ds(pl.multiple_of(2 * clips * lat_rows + clip * 16, 16), 16)
        heads = joined * inner // HEAD_DIM
        for start in range(0, parts, joined):
            ks = range(start, start + joined)
            beside = lambda values: jnp.concatenate(values, axis=1) if joined > 1 else values[0]
            high = beside([shared[k][rows] for k in ks])
            low = beside([shared[k][low_rows] for k in ks])
            top, inv_total = stat_lanes(beside([shared[k][stat_rows] for k in ks]))
            grad_att_rows = grad_att[rows, start * inner : (start + joined) * inner]
            delta = delta_lanes(grad_att_rows, high, low, heads)
            wide_q = spread(beside([queries[k, clip] for k in ks]).astype(F32), heads).astype(BF16)
            wide_g = spread(grad_att_rows.astype(F32), heads).astype(BF16)
            kv = [dot(normed[...], weights[k, :, inner:], "nn").astype(BF16) for k in ks]
            keys = beside([v[:, :inner] for v in kv])
            values = beside([v[:, inner:] for v in kv])
            _, grad_k, grad_v = back_block(keys, values, kept, wide_q, wide_g, top, inv_total, delta)
            for i, k in enumerate(ks):
                cols = slice(i * inner, (i + 1) * inner)
                part = dot(jnp.concatenate([grad_k[:, cols], grad_v[:, cols]], axis=1), weights[k, :, inner:], "nt")
                if k == 0:
                    back[...] = part
                else:
                    back[...] += part
        along_gain, along_bias = jnp.zeros((1, width), F32), jnp.zeros((1, width), F32)
        for f in range(frames):
            at = slice(f * own, (f + 1) * own)
            grad, u = back[at], unit[at]
            scaled = grad * gains[0:1, :]
            mean = jnp.sum(scaled, axis=-1, keepdims=True) * (1.0 / width)
            along = jnp.sum(scaled * u, axis=-1, keepdims=True) * (1.0 / width)
            shifted = inv[at] * (scaled - mean - u * along)
            grad_out[0, f] = shifted.astype(BF16)
            sums_out[pl.ds(first + f, 1), :] += jnp.sum(shifted, axis=0, keepdims=True)
            along_gain += jnp.sum(grad * u, axis=0, keepdims=True)
            along_bias += jnp.sum(grad, axis=0, keepdims=True)
        total_frames = frames * pl.num_programs(1)
        sums_out[total_frames : total_frames + 1] += along_gain
        sums_out[total_frames + 1 : total_frames + 2] += along_bias


def own_patches_back(counts, place, media, time_embed, gains, weights, queries, grad_att, shared):
    clips, frames, patches, width = media.shape
    parts = len(shared)
    own = patches // parts
    lat_rows, inner = queries.shape[2:]
    some = min(FRAME_GROUP, frames)
    full = lambda *shape: pl.BlockSpec(shape, lambda c, g, s: (0,) * len(shape), pipeline_mode=pl.Buffered(1))
    return pl.pallas_call(
        own_patches_kernel,
        grid_spec=pltpu.PrefetchScalarGridSpec(
            num_scalar_prefetch=1,
            grid=(clips, frames // some),
            in_specs=[
                pl.BlockSpec((1, some, own, width), lambda c, g, s: (c, g, s[clips], 0)),
                full(frames, width),
                full(2, width),
                full(*weights.shape),
                full(*queries.shape),
                full(*grad_att.shape),
            ]
            + [full(*shared[0].shape)] * parts,
            out_specs=[
                pl.BlockSpec((1, some, own, width), lambda c, g, s: (c, g, 0, 0)),
                pl.BlockSpec((16, width), lambda c, g, s: (0, 0)),
            ],
            scratch_shapes=[
                pltpu.VMEM((some * own, width), F32),
                pltpu.VMEM((some * own, 1), F32),
                pltpu.VMEM((some * own, width), BF16),
                pltpu.VMEM((some * own, width), F32),
            ],
        ),
        out_shape=[
            jax.ShapeDtypeStruct((clips, frames, own, width), BF16),
            jax.ShapeDtypeStruct((16, width), F32),
        ],
        compiler_params=pltpu.CompilerParams(vmem_limit_bytes=56 << 20),
        cost_estimate=pl.CostEstimate(
            flops=6 * clips * frames * own * width * 2 * inner * parts,
            bytes_accessed=4 * clips * frames * own * width,
            transcendentals=0,
        ),
    )(jnp.concatenate([counts, place[None]]), media, time_embed, gains, weights, queries, grad_att, *shared)


def body(
    latents_in, media_tokens, frame_counts, time_embed, media_gain, media_bias, latent_gain, latent_bias,
    ff_gain, ff_bias, w_query, w_key, w_value, w_out, w_up, w_down, cotangent,
):
    clips, frames, patches, width = media_tokens.shape
    lat_rows = latents_in.shape[1]
    inner = w_query.shape[1]
    parts = lax.axis_size("heads")
    place = lax.axis_index("heads")
    dp_size = lax.axis_size("dp")
    rows = clips * lat_rows
    time32 = time_embed.astype(F32)
    media_gains = jnp.stack([media_gain, media_bias]).astype(F32)
    all_gains = jnp.stack([media_gain, media_bias, latent_gain, latent_bias]).astype(F32)
    ff_gains = jnp.stack([ff_gain, ff_bias]).astype(F32)

    high_bit = dp_size.bit_length() - 2
    w_qkv = jnp.concatenate([w_query, w_key, w_value], axis=1)
    out_all = gather_weight(w_out, [0]).reshape(parts * inner, width)
    qkv_all = gather_weight(w_qkv, [high_bit, 0])

    kv, normed_lat, queries, shared = forward_own(
        latents_in, media_tokens, frame_counts, time32, all_gains, w_query, w_qkv[:, inner:]
    )
    shared_all = from_all(shared, "heads")
    cot_rows = cotangent.reshape(rows, width)
    normed_ff, active, grad_hidden, latents_out, grad_mixed, branch, grad_att, ff_sums = feed(
        latents_in.reshape(rows, width), shared_all, cot_rows, out_all, ff_gains, w_up, w_down
    )

    side = bit_of("heads", 0)
    up_half = w_up.shape[1] // 2
    down_half = width // 2
    hidden_half = lax.dynamic_slice_in_dim(grad_hidden, side * up_half, up_half, 1)
    cot_half = lax.dynamic_slice_in_dim(cot_rows, side * down_half, down_half, 1)
    grad_up = mm("rd,rf->df", normed_ff, hidden_half).astype(BF16)
    grad_down = mm("rf,rd->fd", active, cot_half).astype(BF16)
    order_a, order_b = dp_orders()
    up_sum = scatter_sum(grad_up.reshape(dp_size, -1, up_half), order_a).astype(BF16)
    down_sum = scatter_sum(grad_down.reshape(dp_size, -1, down_half), order_b).astype(BF16)
    grad_up_own = side_by_side(up_sum, swap(up_sum, "heads", 1), "heads", 0, 1).reshape(len(up_sum), -1).astype(F32)
    grad_down_own = side_by_side(down_sum, swap(down_sum, "heads", 1), "heads", 0, 1).reshape(len(down_sum), -1).astype(F32)

    lat_grads, weight_part = own_heads_back(
        frame_counts, media_tokens, kv, time32, media_gains, normed_lat, queries, shared, grad_att, branch, dp_size
    )
    weight_sum = gather_dp_blocks(scatter_sum(weight_part, order_a).astype(BF16), order_a[::-1]).astype(F32)
    if width // dp_size != inner:
        weight_qkv = weight_sum[:, : 3 * inner].reshape(dp_size, 3, inner, -1).transpose(1, 0, 3, 2)
    else:
        weight_qkv = weight_sum[:, : 3 * inner].reshape(dp_size, 3, inner, inner).transpose(1, 0, 2, 3)
    grad_query, grad_key, grad_value = (weight_qkv[i].reshape(width, inner) for i in range(3))
    grad_out = weight_sum[:, 3 * inner :].transpose(1, 0, 2).reshape(inner, width)

    query_all = (mm("crd,kdi->kcri", normed_lat, qkv_all[:, :, :inner]) * HEAD_DIM**-0.5).astype(BF16)
    grad_media, media_sums = own_patches_back(
        frame_counts, place, media_tokens, time32, media_gains, qkv_all, query_all, grad_att, shared_all
    )

    lat_all = jnp.stack(from_all(lat_grads, "heads"))
    lat_back = mm("kri,kdi->rd", lat_all, qkv_all)
    latents = latents_in.reshape(rows, width).astype(F32)
    lat_unit, lat_inv = normalised(latents)
    grad_latents = (grad_mixed + norm_back(lat_back, lat_unit, lat_inv, all_gains[2])).astype(BF16)

    def rows_sum(values):
        return jnp.sum(values, axis=0, keepdims=True) / parts

    small = sum_all(
        jnp.concatenate(
            [media_sums[: frames + 2], rows_sum(lat_back * lat_unit), rows_sum(lat_back), ff_sums[:2] / parts]
        )
    )
    return (
        latents_out.reshape(latents_in.shape),
        grad_latents.reshape(latents_in.shape),
        grad_media,
        small[:frames],
        *(small[frames + i] for i in range(6)),
        grad_query,
        grad_key,
        grad_value,
        grad_out,
        grad_up_own,
        grad_down_own,
    )


def solution(mesh):
    clip, whole, column = P("dp", None, None), P(), P(None, "heads")
    media = P("dp", None, None, None)
    placed = (clip, media, P("dp")) + (whole,) * 7 + (column,) * 3 + (P("heads", None), whole, whole, clip)
    return jax.shard_map(
        body,
        mesh=mesh,
        in_specs=placed,
        out_specs=(clip, clip, P("dp", None, "heads", None))
        + (whole,) * 7
        + (column,) * 3
        + (P("heads", None), P("dp", None), P("dp", None)),
        check_vma=False,
    )
```
